32 devices in a mesh: gx: 8 (over z, core), gy: 4 (over y, x).
Axes of the slice: x: 2, y: 2, z: 4, core: 2. Of those that a mesh axis runs over, the one named last changes fastest.
Arguments:
- tokens: bfloat16 [256, 16384], P('gy', 'gx'), may hold values from -6 to 6
- gate_weight: bfloat16 [16384, 26624], P('gx', 'gy'), may hold values from -0.046875 to 0.046875
- up_weight: bfloat16 [16384, 26624], P('gx', 'gy'), may hold values from -0.046875 to 0.046875
- down_weight: bfloat16 [26624, 16384], P('gy', 'gx'), may hold values from -0.0390625 to 0.0390625
Outputs:
- mixed: float32 [256, 16384], P('gy', 'gx')
The draws below stay inside these ranges and needn't reach their ends.
All inputs are finite; a program needn't handle non-finite values.
Results may differ from the reference program's by a relative error of at most 0.0029.
Values may be sent and summed in bfloat16 or wider, within the bound.
No kernel may reach another device: no remote copies, remote signals or barrier semaphores. Data moves between devices by JAX's collectives and lax.ppermute only.
A program may use at most 192 MiB of HBM per device.

```python
import jax
import jax.numpy as jnp

D = 16384
FFW = 26624
TOKENS = 256


def block_scale(key, shape, pieces, least, high):
    factor_of = 1.0
    for axis_at, shards_of in pieces:
        draws = jax.random.uniform(jax.random.fold_in(jax.random.fold_in(key, 6), axis_at), (shards_of,), jnp.float32, least / len(pieces), high / len(pieces))
        factor_of = factor_of * jnp.repeat(jnp.exp(draws), shape[axis_at] // shards_of).reshape((-1,) + (1,) * (len(shape) - 1 - axis_at))
    return factor_of


def scatter_about(rng, extent, spread, reach, split=(), dtype=jnp.bfloat16):
    factor_of = block_scale(rng, extent, split, -0.22, 0.18) if split else 1.0
    array = jax.random.normal(rng, extent, jnp.float32) * spread * factor_of
    return jnp.minimum(jnp.maximum(array, -reach), reach).astype(dtype)


def setup_inputs(seed: int = 0) -> dict:
    seeds = jax.random.split(jax.random.key(seed), 5)
    tokens = scatter_about(seeds[0], (TOKENS, D), 1.0, 6.0, ((0, 4), (1, 8)))
    gate_weight = scatter_about(seeds[1], (D, FFW), D ** -0.5, 0.046875, ((0, 8), (1, 4)))
    up_weight = scatter_about(seeds[2], (D, FFW), D ** -0.5, 0.046875, ((0, 8), (1, 4)))
    down_weight = scatter_about(seeds[3], (FFW, D), FFW ** -0.5, 0.0390625, ((0, 4), (1, 8)))
    return dict(tokens=tokens, gate_weight=gate_weight, up_weight=up_weight, down_weight=down_weight)


def reference(tokens, gate_weight, up_weight, down_weight):
    gate = jnp.dot(tokens, gate_weight, preferred_element_type=jnp.float32)
    up = jnp.dot(tokens, up_weight, preferred_element_type=jnp.float32)
    hidden = (jax.nn.silu(gate) * up).astype(jnp.bfloat16)
    return jnp.dot(hidden, down_weight, preferred_element_type=jnp.float32)
```

```python
import functools
import math

import jax
import jax.numpy as jnp
from jax import lax
from jax.experimental import pallas as pl
from jax.experimental.pallas import tpu as pltpu
from jax.sharding import PartitionSpec as P

CORES = 2
TOKEN_MAX = 6.0
WEIGHT_MAX = 0.046875
VMEM = 40 * 1024 * 1024
PIECES = 2
SIZES = [3, 3, 3, 2, 2]
GAPS = [0, 1, 1, 2]


def encode(v, scale):
    root = lax.rsqrt(jnp.maximum(jnp.abs(v), 1e-37))
    return (v * root * scale).astype(jnp.float16)


def decode(q, scale):
    u = q.astype(jnp.float32)
    return u * jnp.abs(u) * (1.0 / (scale * scale))


def first(rows, gate_weight, up_weight, start, width, tile):
    count, depth = rows.shape
    half = count // 2
    steps = [(k, i) for i in range(width // tile) for k in (0, 1)]
    slots = 3
    piece = depth // PIECES

    def kernel(rows_ref, gate_ref, up_ref, theirs_ref, mine_ref, held, sems):
        def load(n):
            k, i = steps[n]
            ref = (gate_ref, up_ref)[k]
            slot = n % slots
            return [
                pltpu.make_async_copy(
                    ref.at[pl.ds(p * piece, piece), pl.ds(start + i * tile, tile)],
                    held.at[slot, pl.ds(p * piece, piece)],
                    sems.at[slot, p],
                )
                for p in range(PIECES)
            ]

        for n in range(min(slots - 1, len(steps))):
            for copy in load(n):
                copy.start()
        for n, (k, i) in enumerate(steps):
            if n + slots - 1 < len(steps):
                for copy in load(n + slots - 1):
                    copy.start()
            for copy in load(n):
                copy.wait()
            part = jnp.dot(rows_ref[...], held[n % slots], preferred_element_type=jnp.float32)
            theirs_ref[k, :, i * tile : (i + 1) * tile] = part[:half]
            mine_ref[k, :, i * tile : (i + 1) * tile] = part[half:]

    hbm = pl.BlockSpec(memory_space=pltpu.HBM)
    vmem = pl.BlockSpec(memory_space=pltpu.VMEM)
    shape = pltpu.VMEM((2, half, width), jnp.float32)
    return pl.pallas_call(
        kernel,
        in_specs=[vmem, hbm, hbm],
        out_specs=[vmem, vmem],
        out_shape=[shape, shape],
        scratch_shapes=[
            pltpu.VMEM((slots, depth, tile), jnp.bfloat16),
            pltpu.SemaphoreType.DMA((slots, PIECES)),
        ],
        compiler_params=pltpu.CompilerParams(vmem_limit_bytes=VMEM),
        cost_estimate=pl.CostEstimate(
            flops=4 * count * depth * width,
            bytes_accessed=4 * depth * width + 8 * count * width,
            transcendentals=0,
        ),
    )(rows, gate_weight, up_weight)


def second(total, parts, down_weight, start, width, tile):
    half = parts[0].shape[0]
    depth = down_weight.shape[1]
    carried = total is not None
    slots = 3
    steps = depth // tile
    piece = width // PIECES

    def kernel(*refs):
        weight_ref = refs[2]
        out_ref, rows, held, sems = refs[-4:]

        def load(n):
            return [
                pltpu.make_async_copy(
                    weight_ref.at[pl.ds(start + p * piece, piece), pl.ds(n * tile, tile)],
                    held.at[n % slots, pl.ds(p * piece, piece)],
                    sems.at[n % slots, p],
                )
                for p in range(PIECES)
            ]

        for n in range(min(slots - 1, steps)):
            for copy in load(n):
                copy.start()
        rows[:half] = refs[0][...]
        rows[half:] = refs[1][...]
        for n in range(steps):
            if n + slots - 1 < steps:
                for copy in load(n + slots - 1):
                    copy.start()
            for copy in load(n):
                copy.wait()
            part = jnp.dot(rows[...], held[n % slots], preferred_element_type=jnp.float32)
            at = slice(n * tile, (n + 1) * tile)
            if carried:
                part = part + refs[3][:, at]
            out_ref[:, at] = part

    hbm = pl.BlockSpec(memory_space=pltpu.HBM)
    vmem = pl.BlockSpec(memory_space=pltpu.VMEM)
    return pl.pallas_call(
        kernel,
        in_specs=[vmem, vmem, hbm] + ([vmem] if carried else []),
        out_specs=vmem,
        out_shape=jax.ShapeDtypeStruct((2 * half, depth), jnp.float32),
        scratch_shapes=[
            pltpu.VMEM((2 * half, width), jnp.bfloat16),
            pltpu.VMEM((slots, width, tile), jnp.bfloat16),
            pltpu.SemaphoreType.DMA((slots, PIECES)),
        ],
        compiler_params=pltpu.CompilerParams(vmem_limit_bytes=VMEM),
        cost_estimate=pl.CostEstimate(
            flops=4 * half * depth * width,
            bytes_accessed=2 * depth * width + 16 * half * depth,
            transcendentals=0,
        ),
    )(*parts, down_weight, *([total] if carried else []))


def unit_of(width):
    for unit in (512, 256, 128):
        if width % unit == 0:
            return unit
    return width


def plan(count):
    if count == sum(SIZES):
        return SIZES, GAPS
    return [1] * count, [1] * (count - 1)


def queue(steps, gaps):
    waiting, order = [], []

    def take():
        chunk, step = waiting.pop(0)
        order.append((chunk, step))
        if step + 1 < steps:
            waiting.append((chunk, step + 1))

    for chunk in range(len(gaps) + 1):
        for _ in range(gaps[chunk - 1] if chunk else 0):
            if waiting:
                take()
        order.append((chunk, 0))
        waiting.append((chunk, 1))
    while waiting:
        take()
    return order


def local(tokens, gate_weight, up_weight, down_weight, *, n_gx, n_gy):
    chips = n_gx // CORES
    own, depth = tokens.shape
    width = gate_weight.shape[1]
    x = lax.axis_index("gx")
    y = lax.axis_index("gy")
    z, core = x // CORES, x % CORES
    half = own * n_gy // CORES
    per = n_gy // CORES
    away = jnp.where(core == 0, z, chips - 1 - z)

    limit = TOKEN_MAX * WEIGHT_MAX * depth * n_gx
    scale = 2.0 ** math.floor(math.log2(60000.0 / math.sqrt(limit)))

    def swap(v):
        return lax.ppermute(v, "gx", [(i, i ^ 1) for i in range(n_gx)])

    def towards(v, step):
        return lax.ppermute(
            v,
            "gx",
            [
                ((chips - step) * CORES, (chips - step - 1) * CORES),
                ((step - 1) * CORES + 1, step * CORES + 1),
            ],
        )

    def back(v, step):
        return lax.ppermute(
            v,
            "gx",
            [
                ((step - 1) * CORES, step * CORES),
                ((chips - step) * CORES + 1, (chips - step - 1) * CORES + 1),
            ],
        )

    def across(v, shift):
        return lax.ppermute(v, "gy", [(i, i ^ shift) for i in range(n_gy)])

    blocks = jnp.stack([tokens] + [across(tokens, s) for s in range(1, n_gy)])
    rows = jnp.concatenate(
        [
            lax.dynamic_index_in_dim(blocks, (side * per + b) ^ y, 0, False)
            for side in (1 - core, core)
            for b in range(per)
        ]
    )

    unit = unit_of(width)
    tile = unit
    down_tile = min(depth, 512)
    counts, gaps = plan(width // unit)
    sizes = [n * unit for n in counts]
    starts = [sum(sizes[:c]) for c in range(len(sizes))]

    state = {}
    token = [rows]

    def tied(*values):
        return lax.optimization_barrier(values + (token[0],))[:-1]

    def matmul_in(c):
        (lhs,) = tied(rows)
        theirs, mine = first(lhs, gate_weight, up_weight, starts[c], sizes[c], tile)
        state["mine", c], state["moved", c] = mine, swap(theirs)
        token[0] = mine

    def leave(c):
        mine, got = tied(state["mine", c], state["moved", c])
        held = mine + got
        sent = encode(held, scale)
        state["held", c], state["moved", c] = held, towards(sent, 1)
        token[0] = sent

    def pass_sum(step):
        def run(c):
            held, got = tied(state["held", c], state["moved", c])
            sent = encode(held + decode(got, scale), scale)
            state["moved", c] = towards(sent, step + 1)
            token[0] = sent

        return run

    def finish(c):
        held, got = tied(state["held", c], state["moved", c])
        value = held + decode(got, scale)
        hidden = (jax.nn.silu(value[0]) * value[1]).astype(jnp.bfloat16)
        state["stage", c], state["moved", c] = [hidden], back(hidden, 1)
        token[0] = hidden

    def pass_hidden(step):
        def run(c):
            (got,) = tied(state["moved", c])
            state["stage", c].append(got)
            state["moved", c] = back(got, step + 1)
            token[0] = got

        return run

    def gather(c):
        (got,) = tied(state["moved", c])
        rows_here = got
        for step, stage in enumerate(state["stage", c]):
            rows_here = jnp.where(away == step, stage, rows_here)
        state["parts", c], state["moved", c] = rows_here, swap(rows_here)
        token[0] = rows_here

    def matmul_out(c):
        parts = tied(state["parts", c], state["moved", c])
        token[0] = state["total"] = second(
            state.get("total"), parts, down_weight, starts[c], sizes[c], down_tile
        )

    steps = [matmul_in, leave]
    steps += [pass_sum(step) for step in range(1, chips - 1)]
    steps += [finish]
    steps += [pass_hidden(step) for step in range(1, chips - 1)]
    steps += [gather, matmul_out]
    for chunk, step in queue(len(steps), gaps):
        steps[step](chunk)
    total = state["total"]

    def block_for(j):
        at = ((j // per) ^ core) * half + (j % per) * own
        return lax.dynamic_slice_in_dim(total, at, own, 0)

    result = block_for(y)
    for shift in range(1, n_gy):
        result = result + across(block_for(y ^ shift).astype(jnp.bfloat16), shift).astype(jnp.float32)
    return result


def solution(mesh):
    n_gx, n_gy = mesh.shape["gx"], mesh.shape["gy"]
    placed = (P("gy", "gx"), P("gx", "gy"), P("gx", "gy"), P("gy", "gx"))
    return jax.shard_map(
        functools.partial(local, n_gx=n_gx, n_gy=n_gy),
        mesh=mesh,
        in_specs=placed,
        out_specs=P("gy", "gx"),
        check_vma=False,
    )
```

```python
import functools
import math

import jax
import jax.numpy as jnp
from jax import lax
from jax.experimental import pallas as pl
from jax.experimental.pallas import tpu as pltpu
from jax.sharding import PartitionSpec as P

CORES = 2
TOKEN_MAX = 6.0
WEIGHT_MAX = 0.046875
VMEM = 20 * 1024 * 1024
PIECES = 2
SIZES = [3, 3, 2, 3, 2]
GAPS = [0, 1, 1, 2]


def encode(v, scale):
    root = lax.rsqrt(jnp.maximum(jnp.abs(v), 1e-37))
    return (v * root * scale).astype(jnp.float16)


def decode(q, scale):
    u = q.astype(jnp.float32)
    return u * jnp.abs(u) * (1.0 / (scale * scale))


def first(rows, gate_weight, up_weight, start, width, tile):
    count, depth = rows.shape
    half = count // 2
    steps = [(k, i) for i in range(width // tile) for k in (0, 1)]
    slots = 3
    piece = depth // PIECES

    def kernel(rows_ref, gate_ref, up_ref, theirs_ref, mine_ref, held, sems):
        def load(n):
            k, i = steps[n]
            ref = (gate_ref, up_ref)[k]
            slot = n % slots
            return [
                pltpu.make_async_copy(
                    ref.at[pl.ds(p * piece, piece), pl.ds(start + i * tile, tile)],
                    held.at[slot, pl.ds(p * piece, piece)],
                    sems.at[slot, p],
                )
                for p in range(PIECES)
            ]

        for n in range(min(slots - 1, len(steps))):
            for copy in load(n):
                copy.start()
        for n, (k, i) in enumerate(steps):
            if n + slots - 1 < len(steps):
                for copy in load(n + slots - 1):
                    copy.start()
            for copy in load(n):
                copy.wait()
            part = jnp.dot(rows_ref[...], held[n % slots], preferred_element_type=jnp.float32)
            theirs_ref[k, :, i * tile : (i + 1) * tile] = part[:half]
            mine_ref[k, :, i * tile : (i + 1) * tile] = part[half:]

    hbm = pl.BlockSpec(memory_space=pltpu.HBM)
    vmem = pl.BlockSpec(memory_space=pltpu.VMEM)
    shape = pltpu.VMEM((2, half, width), jnp.float32)
    return pl.pallas_call(
        kernel,
        in_specs=[vmem, hbm, hbm],
        out_specs=[vmem, vmem],
        out_shape=[shape, shape],
        scratch_shapes=[
            pltpu.VMEM((slots, depth, tile), jnp.bfloat16),
            pltpu.SemaphoreType.DMA((slots, PIECES)),
        ],
        compiler_params=pltpu.CompilerParams(vmem_limit_bytes=VMEM),
        cost_estimate=pl.CostEstimate(
            flops=4 * count * depth * width,
            bytes_accessed=4 * depth * width + 8 * count * width,
            transcendentals=0,
        ),
    )(rows, gate_weight, up_weight)


def second(total, parts, down_weight, start, width, tile):
    half = parts[0].shape[0]
    depth = down_weight.shape[1]
    carried = total is not None
    slots = 3
    steps = depth // tile
    piece = width // PIECES

    def kernel(*refs):
        weight_ref = refs[2]
        out_ref, rows, held, sems = refs[-4:]

        def load(n):
            return [
                pltpu.make_async_copy(
                    weight_ref.at[pl.ds(start + p * piece, piece), pl.ds(n * tile, tile)],
                    held.at[n % slots, pl.ds(p * piece, piece)],
                    sems.at[n % slots, p],
                )
                for p in range(PIECES)
            ]

        for n in range(min(slots - 1, steps)):
            for copy in load(n):
                copy.start()
        rows[:half] = refs[0][...]
        rows[half:] = refs[1][...]
        for n in range(steps):
            if n + slots - 1 < steps:
                for copy in load(n + slots - 1):
                    copy.start()
            for copy in load(n):
                copy.wait()
            part = jnp.dot(rows[...], held[n % slots], preferred_element_type=jnp.float32)
            at = slice(n * tile, (n + 1) * tile)
            if carried:
                part = part + refs[3][:, at]
            out_ref[:, at] = part

    hbm = pl.BlockSpec(memory_space=pltpu.HBM)
    vmem = pl.BlockSpec(memory_space=pltpu.VMEM)
    return pl.pallas_call(
        kernel,
        in_specs=[vmem, vmem, hbm] + ([vmem] if carried else []),
        out_specs=vmem,
        out_shape=jax.ShapeDtypeStruct((2 * half, depth), jnp.float32),
        scratch_shapes=[
            pltpu.VMEM((2 * half, width), jnp.bfloat16),
            pltpu.VMEM((slots, width, tile), jnp.bfloat16),
            pltpu.SemaphoreType.DMA((slots, PIECES)),
        ],
        compiler_params=pltpu.CompilerParams(vmem_limit_bytes=VMEM),
        cost_estimate=pl.CostEstimate(
            flops=4 * half * depth * width,
            bytes_accessed=2 * depth * width + 16 * half * depth,
            transcendentals=0,
        ),
    )(*parts, down_weight, *([total] if carried else []))


def unit_of(width):
    for unit in (512, 256, 128):
        if width % unit == 0:
            return unit
    return width


def plan(count):
    if count == sum(SIZES):
        return SIZES, GAPS
    return [1] * count, [1] * (count - 1)


def queue(steps, gaps):
    waiting, order = [], []

    def take():
        chunk, step = waiting.pop(0)
        order.append((chunk, step))
        if step + 1 < steps:
            waiting.append((chunk, step + 1))

    for chunk in range(len(gaps) + 1):
        for _ in range(gaps[chunk - 1] if chunk else 0):
            if waiting:
                take()
        order.append((chunk, 0))
        waiting.append((chunk, 1))
    while waiting:
        take()
    return order


def local(tokens, gate_weight, up_weight, down_weight, *, n_gx, n_gy):
    chips = n_gx // CORES
    own, depth = tokens.shape
    width = gate_weight.shape[1]
    gate_weight, up_weight, down_weight = (
        pltpu.with_memory_space_constraint(w, pltpu.HBM)
        for w in (gate_weight, up_weight, down_weight)
    )
    x = lax.axis_index("gx")
    y = lax.axis_index("gy")
    z, core = x // CORES, x % CORES
    half = own * n_gy // CORES
    per = n_gy // CORES
    away = jnp.where(core == 0, z, chips - 1 - z)

    limit = TOKEN_MAX * WEIGHT_MAX * depth * n_gx
    scale = 2.0 ** math.floor(math.log2(60000.0 / math.sqrt(limit)))

    def swap(v):
        return lax.ppermute(v, "gx", [(i, i ^ 1) for i in range(n_gx)])

    def hop(v, pairs):
        idle = set(range(n_gx)) - {i for pair in pairs for i in pair}
        return lax.ppermute(v, "gx", pairs + [(i, i) for i in sorted(idle)])

    def towards(v, step):
        return hop(
            v,
            [
                ((chips - step) * CORES, (chips - step - 1) * CORES),
                ((step - 1) * CORES + 1, step * CORES + 1),
            ],
        )

    def back(v, step):
        return hop(
            v,
            [
                ((step - 1) * CORES, step * CORES),
                ((chips - step) * CORES + 1, (chips - step - 1) * CORES + 1),
            ],
        )

    def across(v, shift):
        return lax.ppermute(v, "gy", [(i, i ^ shift) for i in range(n_gy)])

    blocks = jnp.stack([tokens] + [across(tokens, s) for s in range(1, n_gy)])
    rows = jnp.concatenate(
        [
            lax.dynamic_index_in_dim(blocks, (side * per + b) ^ y, 0, False)
            for side in (1 - core, core)
            for b in range(per)
        ]
    )

    unit = unit_of(width)
    tile = unit
    down_tile = min(depth, 512)
    counts, gaps = plan(width // unit)
    sizes = [n * unit for n in counts]
    starts = [sum(sizes[:c]) for c in range(len(sizes))]

    state = {}
    token = [rows]

    def tied(*values):
        return lax.optimization_barrier(values + (token[0],))[:-1]

    def matmul_in(c):
        (lhs,) = tied(rows)
        theirs, mine = first(lhs, gate_weight, up_weight, starts[c], sizes[c], tile)
        state["mine", c], state["moved", c] = mine, swap(theirs)
        token[0] = mine

    def leave(c):
        mine, got = tied(state["mine", c], state["moved", c])
        held = mine + got
        sent = encode(held, scale)
        state["held", c], state["moved", c] = held, towards(sent, 1)
        token[0] = sent

    def pass_sum(step):
        def run(c):
            held, got = tied(state["held", c], state["moved", c])
            sent = encode(held + decode(got, scale), scale)
            state["moved", c] = towards(sent, step + 1)
            token[0] = sent

        return run

    def finish(c):
        held, got = tied(state["held", c], state["moved", c])
        value = held + decode(got, scale)
        hidden = (jax.nn.silu(value[0]) * value[1]).astype(jnp.bfloat16)
        state["stage", c], state["moved", c] = [hidden], back(hidden, 1)
        token[0] = hidden

    def pass_hidden(step):
        def run(c):
            (got,) = tied(state["moved", c])
            state["stage", c].append(got)
            state["moved", c] = back(got, step + 1)
            token[0] = got

        return run

    def gather(c):
        (got,) = tied(state["moved", c])
        rows_here = got
        for step, stage in enumerate(state["stage", c]):
            rows_here = jnp.where(away == step, stage, rows_here)
        state["parts", c], state["moved", c] = rows_here, swap(rows_here)
        token[0] = rows_here

    def matmul_out(c):
        parts = tied(state["parts", c], state["moved", c])
        token[0] = state["total"] = second(
            state.get("total"), parts, down_weight, starts[c], sizes[c], down_tile
        )

    steps = [matmul_in, leave]
    steps += [pass_sum(step) for step in range(1, chips - 1)]
    steps += [finish]
    steps += [pass_hidden(step) for step in range(1, chips - 1)]
    steps += [gather, matmul_out]
    for chunk, step in queue(len(steps), gaps):
        steps[step](chunk)
    total = state["total"]

    def block_for(j):
        at = ((j // per) ^ core) * half + (j % per) * own
        return lax.dynamic_slice_in_dim(total, at, own, 0)

    result = block_for(y)
    for shift in range(1, n_gy):
        result = result + across(block_for(y ^ shift).astype(jnp.bfloat16), shift).astype(jnp.float32)
    return result


def solution(mesh):
    n_gx, n_gy = mesh.shape["gx"], mesh.shape["gy"]
    placed = (P("gy", "gx"), P("gx", "gy"), P("gx", "gy"), P("gy", "gx"))
    return jax.shard_map(
        functools.partial(local, n_gx=n_gx, n_gy=n_gy),
        mesh=mesh,
        in_specs=placed,
        out_specs=P("gy", "gx"),
        check_vma=False,
    )
```

```python
import functools
import math

import jax
import jax.numpy as jnp
from jax import lax
from jax.experimental import pallas as pl
from jax.experimental.pallas import tpu as pltpu
from jax.sharding import PartitionSpec as P

CORES = 2
TOKEN_MAX = 6.0
WEIGHT_MAX = 0.046875
VMEM = 14 * 1024 * 1024
PIECES = 2
SIZES = [3, 3, 2, 3, 2]
GAPS = [0, 1, 1, 2]


def encode(v, scale):
    root = lax.rsqrt(jnp.maximum(jnp.abs(v), 1e-37))
    return (v * root * scale).astype(jnp.float16)


def decode(q, scale):
    u = q.astype(jnp.float32)
    return u * jnp.abs(u) * (1.0 / (scale * scale))


def first(rows, gate_weight, up_weight, start, width, tile):
    count, depth = rows.shape
    half = count // 2
    steps = [(k, i) for i in range(width // tile) for k in (0, 1)]
    slots = 3
    piece = depth // PIECES

    def kernel(rows_ref, gate_ref, up_ref, theirs_ref, mine_ref, held, sems):
        def load(n):
            k, i = steps[n]
            ref = (gate_ref, up_ref)[k]
            slot = n % slots
            return [
                pltpu.make_async_copy(
                    ref.at[pl.ds(p * piece, piece), pl.ds(start + i * tile, tile)],
                    held.at[slot, pl.ds(p * piece, piece)],
                    sems.at[slot, p],
                )
                for p in range(PIECES)
            ]

        for n in range(min(slots - 1, len(steps))):
            for copy in load(n):
                copy.start()
        for n, (k, i) in enumerate(steps):
            if n + slots - 1 < len(steps):
                for copy in load(n + slots - 1):
                    copy.start()
            for copy in load(n):
                copy.wait()
            part = jnp.dot(rows_ref[...], held[n % slots], preferred_element_type=jnp.float32)
            theirs_ref[k, :, i * tile : (i + 1) * tile] = part[:half]
            mine_ref[k, :, i * tile : (i + 1) * tile] = part[half:]

    hbm = pl.BlockSpec(memory_space=pltpu.HBM)
    vmem = pl.BlockSpec(memory_space=pltpu.VMEM)
    shape = pltpu.VMEM((2, half, width), jnp.float32)
    return pl.pallas_call(
        kernel,
        in_specs=[vmem, hbm, hbm],
        out_specs=[vmem, vmem],
        out_shape=[shape, shape],
        scratch_shapes=[
            pltpu.VMEM((slots, depth, tile), jnp.bfloat16),
            pltpu.SemaphoreType.DMA((slots, PIECES)),
        ],
        compiler_params=pltpu.CompilerParams(vmem_limit_bytes=VMEM),
        cost_estimate=pl.CostEstimate(
            flops=4 * count * depth * width,
            bytes_accessed=4 * depth * width + 8 * count * width,
            transcendentals=0,
        ),
    )(rows, gate_weight, up_weight)


def second(total, parts, down_weight, start, width, tile):
    half = parts[0].shape[0]
    depth = down_weight.shape[1]
    carried = total is not None
    slots = 3
    steps = depth // tile
    piece = width // PIECES

    def kernel(*refs):
        weight_ref = refs[2]
        out_ref, rows, held, sems = refs[-4:]

        def load(n):
            return [
                pltpu.make_async_copy(
                    weight_ref.at[pl.ds(start + p * piece, piece), pl.ds(n * tile, tile)],
                    held.at[n % slots, pl.ds(p * piece, piece)],
                    sems.at[n % slots, p],
                )
                for p in range(PIECES)
            ]

        for n in range(min(slots - 1, steps)):
            for copy in load(n):
                copy.start()
        rows[:half] = refs[0][...]
        rows[half:] = refs[1][...]
        for n in range(steps):
            if n + slots - 1 < steps:
                for copy in load(n + slots - 1):
                    copy.start()
            for copy in load(n):
                copy.wait()
            part = jnp.dot(rows[...], held[n % slots], preferred_element_type=jnp.float32)
            at = slice(n * tile, (n + 1) * tile)
            if carried:
                part = part + refs[3][:, at]
            out_ref[:, at] = part

    hbm = pl.BlockSpec(memory_space=pltpu.HBM)
    vmem = pl.BlockSpec(memory_space=pltpu.VMEM)
    return pl.pallas_call(
        kernel,
        in_specs=[vmem, vmem, hbm] + ([vmem] if carried else []),
        out_specs=vmem,
        out_shape=jax.ShapeDtypeStruct((2 * half, depth), jnp.float32),
        scratch_shapes=[
            pltpu.VMEM((2 * half, width), jnp.bfloat16),
            pltpu.VMEM((slots, width, tile), jnp.bfloat16),
            pltpu.SemaphoreType.DMA((slots, PIECES)),
        ],
        compiler_params=pltpu.CompilerParams(vmem_limit_bytes=VMEM),
        cost_estimate=pl.CostEstimate(
            flops=4 * half * depth * width,
            bytes_accessed=2 * depth * width + 16 * half * depth,
            transcendentals=0,
        ),
    )(*parts, down_weight, *([total] if carried else []))


def unit_of(width):
    for unit in (512, 256, 128):
        if width % unit == 0:
            return unit
    return width


def plan(count):
    if count == sum(SIZES):
        return SIZES, GAPS
    return [1] * count, [1] * (count - 1)


def queue(steps, gaps):
    waiting, order = [], []

    def take():
        chunk, step = waiting.pop(0)
        order.append((chunk, step))
        if step + 1 < steps:
            waiting.append((chunk, step + 1))

    for chunk in range(len(gaps) + 1):
        for _ in range(gaps[chunk - 1] if chunk else 0):
            if waiting:
                take()
        order.append((chunk, 0))
        waiting.append((chunk, 1))
    while waiting:
        take()
    return order


def local(tokens, gate_weight, up_weight, down_weight, *, n_gx, n_gy):
    chips = n_gx // CORES
    own, depth = tokens.shape
    width = gate_weight.shape[1]
    gate_weight, up_weight, down_weight = (
        pltpu.with_memory_space_constraint(w, pltpu.HBM)
        for w in (gate_weight, up_weight, down_weight)
    )
    x = lax.axis_index("gx")
    y = lax.axis_index("gy")
    z, core = x // CORES, x % CORES
    half = own * n_gy // CORES
    per = n_gy // CORES
    away = jnp.where(core == 0, z, chips - 1 - z)

    limit = TOKEN_MAX * WEIGHT_MAX * depth * n_gx
    scale = 2.0 ** math.floor(math.log2(60000.0 / math.sqrt(limit)))

    def swap(v):
        return lax.ppermute(v, "gx", [(i, i ^ 1) for i in range(n_gx)])

    def hop(v, pairs):
        idle = set(range(n_gx)) - {i for pair in pairs for i in pair}
        return lax.ppermute(v, "gx", pairs + [(i, i) for i in sorted(idle)])

    def towards(v, step):
        return hop(
            v,
            [
                ((chips - step) * CORES, (chips - step - 1) * CORES),
                ((step - 1) * CORES + 1, step * CORES + 1),
            ],
        )

    def back(v, step):
        return hop(
            v,
            [
                ((step - 1) * CORES, step * CORES),
                ((chips - step) * CORES + 1, (chips - step - 1) * CORES + 1),
            ],
        )

    def across(v, shift):
        return lax.ppermute(v, "gy", [(i, i ^ shift) for i in range(n_gy)])

    blocks = jnp.stack([tokens] + [across(tokens, s) for s in range(1, n_gy)])
    rows = jnp.concatenate(
        [
            lax.dynamic_index_in_dim(blocks, (side * per + b) ^ y, 0, False)
            for side in (1 - core, core)
            for b in range(per)
        ]
    )

    unit = unit_of(width)
    tile = unit
    down_tile = min(depth, 512)
    counts, gaps = plan(width // unit)
    sizes = [n * unit for n in counts]
    starts = [sum(sizes[:c]) for c in range(len(sizes))]

    state = {}
    token = [rows]

    def tied(*values):
        return lax.optimization_barrier(values + (token[0],))[:-1]

    def matmul_in(c):
        (lhs,) = tied(rows)
        theirs, mine = first(lhs, gate_weight, up_weight, starts[c], sizes[c], tile)
        state["mine", c], state["moved", c] = mine, swap(theirs)
        token[0] = mine

    def leave(c):
        mine, got = tied(state["mine", c], state["moved", c])
        held = mine + got
        sent = encode(held, scale)
        state["held", c], state["moved", c] = held, towards(sent, 1)
        token[0] = sent

    def pass_sum(step):
        def run(c):
            held, got = tied(state["held", c], state["moved", c])
            sent = encode(held + decode(got, scale), scale)
            state["moved", c] = towards(sent, step + 1)
            token[0] = sent

        return run

    def finish(c):
        held, got = tied(state["held", c], state["moved", c])
        value = held + decode(got, scale)
        hidden = (jax.nn.silu(value[0]) * value[1]).astype(jnp.bfloat16)
        state["stage", c], state["moved", c] = [hidden], back(hidden, 1)
        token[0] = hidden

    def pass_hidden(step):
        def run(c):
            (got,) = tied(state["moved", c])
            state["stage", c].append(got)
            state["moved", c] = back(got, step + 1)
            token[0] = got

        return run

    def gather(c):
        (got,) = tied(state["moved", c])
        rows_here = got
        for step, stage in enumerate(state["stage", c]):
            rows_here = jnp.where(away == step, stage, rows_here)
        state["parts", c], state["moved", c] = rows_here, swap(rows_here)
        token[0] = rows_here

    def matmul_out(c):
        parts = tied(state["parts", c], state["moved", c])
        token[0] = state["total"] = second(
            state.get("total"), parts, down_weight, starts[c], sizes[c], down_tile
        )

    steps = [matmul_in, leave]
    steps += [pass_sum(step) for step in range(1, chips - 1)]
    steps += [finish]
    steps += [pass_hidden(step) for step in range(1, chips - 1)]
    steps += [gather, matmul_out]
    for chunk, step in queue(len(steps), gaps):
        steps[step](chunk)
    total = state["total"]

    def block_for(j):
        at = ((j // per) ^ core) * half + (j % per) * own
        return lax.dynamic_slice_in_dim(total, at, own, 0)

    result = block_for(y)
    for shift in range(1, n_gy):
        result = result + across(block_for(y ^ shift).astype(jnp.bfloat16), shift).astype(jnp.float32)
    return result


def solution(mesh):
    n_gx, n_gy = mesh.shape["gx"], mesh.shape["gy"]
    placed = (P("gy", "gx"), P("gx", "gy"), P("gx", "gy"), P("gy", "gx"))
    return jax.shard_map(
        functools.partial(local, n_gx=n_gx, n_gy=n_gy),
        mesh=mesh,
        in_specs=placed,
        out_specs=P("gy", "gx"),
        check_vma=False,
    )
```

```python
import functools
import math

import jax
import jax.numpy as jnp
from jax import lax
from jax.experimental import pallas as pl
from jax.experimental.pallas import tpu as pltpu
from jax.sharding import PartitionSpec as P

CORES = 2
TOKEN_MAX = 6.0
WEIGHT_MAX = 0.046875
VMEM = 14 * 1024 * 1024
PIECES = 2
SIZES = [2, 2, 3, 3, 3]
GAPS = [0, 1, 1, 2]


def encode(v, scale):
    root = lax.rsqrt(jnp.maximum(jnp.abs(v), 1e-37))
    return (v * root * scale).astype(jnp.float16)


def decode(q, scale):
    u = q.astype(jnp.float32)
    return u * jnp.abs(u) * (1.0 / (scale * scale))


def first(rows, gate_weight, up_weight, start, width, tile):
    count, depth = rows.shape
    half = count // 2
    steps = [(k, i) for i in range(width // tile) for k in (0, 1)]
    slots = 3
    piece = depth // PIECES

    def kernel(rows_ref, gate_ref, up_ref, theirs_ref, mine_ref, held, sems):
        def load(n):
            k, i = steps[n]
            ref = (gate_ref, up_ref)[k]
            slot = n % slots
            return [
                pltpu.make_async_copy(
                    ref.at[pl.ds(p * piece, piece), pl.ds(start + i * tile, tile)],
                    held.at[slot, pl.ds(p * piece, piece)],
                    sems.at[slot, p],
                )
                for p in range(PIECES)
            ]

        for n in range(min(slots - 1, len(steps))):
            for copy in load(n):
                copy.start()
        for n, (k, i) in enumerate(steps):
            if n + slots - 1 < len(steps):
                for copy in load(n + slots - 1):
                    copy.start()
            for copy in load(n):
                copy.wait()
            part = jnp.dot(rows_ref[...], held[n % slots], preferred_element_type=jnp.float32)
            theirs_ref[k, :, i * tile : (i + 1) * tile] = part[:half]
            mine_ref[k, :, i * tile : (i + 1) * tile] = part[half:]

    hbm = pl.BlockSpec(memory_space=pltpu.HBM)
    vmem = pl.BlockSpec(memory_space=pltpu.VMEM)
    shape = pltpu.VMEM((2, half, width), jnp.float32)
    return pl.pallas_call(
        kernel,
        in_specs=[vmem, hbm, hbm],
        out_specs=[vmem, vmem],
        out_shape=[shape, shape],
        scratch_shapes=[
            pltpu.VMEM((slots, depth, tile), jnp.bfloat16),
            pltpu.SemaphoreType.DMA((slots, PIECES)),
        ],
        compiler_params=pltpu.CompilerParams(vmem_limit_bytes=VMEM),
        cost_estimate=pl.CostEstimate(
            flops=4 * count * depth * width,
            bytes_accessed=4 * depth * width + 8 * count * width,
            transcendentals=0,
        ),
    )(rows, gate_weight, up_weight)


def second(total, parts, down_weight, start, width, tile):
    half = parts[0].shape[0]
    depth = down_weight.shape[1]
    carried = total is not None
    slots = 3
    steps = depth // tile
    piece = width // PIECES

    def kernel(*refs):
        weight_ref = refs[2]
        out_ref, rows, held, sems = refs[-4:]

        def load(n):
            return [
                pltpu.make_async_copy(
                    weight_ref.at[pl.ds(start + p * piece, piece), pl.ds(n * tile, tile)],
                    held.at[n % slots, pl.ds(p * piece, piece)],
                    sems.at[n % slots, p],
                )
                for p in range(PIECES)
            ]

        for n in range(min(slots - 1, steps)):
            for copy in load(n):
                copy.start()
        rows[:half] = refs[0][...]
        rows[half:] = refs[1][...]
        for n in range(steps):
            if n + slots - 1 < steps:
                for copy in load(n + slots - 1):
                    copy.start()
            for copy in load(n):
                copy.wait()
            part = jnp.dot(rows[...], held[n % slots], preferred_element_type=jnp.float32)
            at = slice(n * tile, (n + 1) * tile)
            if carried:
                part = part + refs[3][:, at]
            out_ref[:, at] = part

    hbm = pl.BlockSpec(memory_space=pltpu.HBM)
    vmem = pl.BlockSpec(memory_space=pltpu.VMEM)
    return pl.pallas_call(
        kernel,
        in_specs=[vmem, vmem, hbm] + ([vmem] if carried else []),
        out_specs=vmem,
        out_shape=jax.ShapeDtypeStruct((2 * half, depth), jnp.float32),
        scratch_shapes=[
            pltpu.VMEM((2 * half, width), jnp.bfloat16),
            pltpu.VMEM((slots, width, tile), jnp.bfloat16),
            pltpu.SemaphoreType.DMA((slots, PIECES)),
        ],
        compiler_params=pltpu.CompilerParams(vmem_limit_bytes=VMEM),
        cost_estimate=pl.CostEstimate(
            flops=4 * half * depth * width,
            bytes_accessed=2 * depth * width + 16 * half * depth,
            transcendentals=0,
        ),
    )(*parts, down_weight, *([total] if carried else []))


def unit_of(width):
    for unit in (512, 256, 128):
        if width % unit == 0:
            return unit
    return width


def plan(count):
    if count == sum(SIZES):
        return SIZES, GAPS
    return [1] * count, [1] * (count - 1)


def queue(steps, gaps):
    waiting, order = [], []

    def take():
        chunk, step = waiting.pop(0)
        order.append((chunk, step))
        if step + 1 < steps:
            waiting.append((chunk, step + 1))

    for chunk in range(len(gaps) + 1):
        for _ in range(gaps[chunk - 1] if chunk else 0):
            if waiting:
                take()
        order.append((chunk, 0))
        waiting.append((chunk, 1))
    while waiting:
        take()
    return order


def local(tokens, gate_weight, up_weight, down_weight, *, n_gx, n_gy):
    chips = n_gx // CORES
    own, depth = tokens.shape
    width = gate_weight.shape[1]
    gate_weight, up_weight, down_weight = (
        pltpu.with_memory_space_constraint(w, pltpu.HBM)
        for w in (gate_weight, up_weight, down_weight)
    )
    x = lax.axis_index("gx")
    y = lax.axis_index("gy")
    z, core = x // CORES, x % CORES
    half = own * n_gy // CORES
    per = n_gy // CORES
    away = jnp.where(core == 0, z, chips - 1 - z)

    limit = TOKEN_MAX * WEIGHT_MAX * depth * n_gx
    scale = 2.0 ** math.floor(math.log2(60000.0 / math.sqrt(limit)))

    def swap(v):
        return lax.ppermute(v, "gx", [(i, i ^ 1) for i in range(n_gx)])

    def hop(v, pairs):
        idle = set(range(n_gx)) - {i for pair in pairs for i in pair}
        return lax.ppermute(v, "gx", pairs + [(i, i) for i in sorted(idle)])

    def towards(v, step):
        return hop(
            v,
            [
                ((chips - step) * CORES, (chips - step - 1) * CORES),
                ((step - 1) * CORES + 1, step * CORES + 1),
            ],
        )

    def back(v, step):
        return hop(
            v,
            [
                ((step - 1) * CORES, step * CORES),
                ((chips - step) * CORES + 1, (chips - step - 1) * CORES + 1),
            ],
        )

    def across(v, shift):
        return lax.ppermute(v, "gy", [(i, i ^ shift) for i in range(n_gy)])

    blocks = jnp.stack([tokens] + [across(tokens, s) for s in range(1, n_gy)])
    rows = jnp.concatenate(
        [
            lax.dynamic_index_in_dim(blocks, (side * per + b) ^ y, 0, False)
            for side in (1 - core, core)
            for b in range(per)
        ]
    )

    unit = unit_of(width)
    tile = unit
    down_tile = min(depth, 512)
    counts, gaps = plan(width // unit)
    sizes = [n * unit for n in counts]
    starts = [sum(sizes[:c]) for c in range(len(sizes))]

    state = {}
    token = [rows]

    def tied(*values):
        return lax.optimization_barrier(values + (token[0],))[:-1]

    def matmul_in(c):
        (lhs,) = tied(rows)
        theirs, mine = first(lhs, gate_weight, up_weight, starts[c], sizes[c], tile)
        state["mine", c], state["moved", c] = mine, swap(theirs)
        token[0] = mine

    def leave(c):
        mine, got = tied(state["mine", c], state["moved", c])
        held = mine + got
        sent = encode(held, scale)
        state["held", c], state["moved", c] = held, towards(sent, 1)
        token[0] = sent

    def pass_sum(step):
        def run(c):
            held, got = tied(state["held", c], state["moved", c])
            sent = encode(held + decode(got, scale), scale)
            state["moved", c] = towards(sent, step + 1)
            token[0] = sent

        return run

    def finish(c):
        held, got = tied(state["held", c], state["moved", c])
        value = held + decode(got, scale)
        hidden = (jax.nn.silu(value[0]) * value[1]).astype(jnp.bfloat16)
        state["stage", c], state["moved", c] = [hidden], back(hidden, 1)
        token[0] = hidden

    def pass_hidden(step):
        def run(c):
            (got,) = tied(state["moved", c])
            state["stage", c].append(got)
            state["moved", c] = back(got, step + 1)
            token[0] = got

        return run

    def gather(c):
        (got,) = tied(state["moved", c])
        rows_here = got
        for step, stage in enumerate(state["stage", c]):
            rows_here = jnp.where(away == step, stage, rows_here)
        state["parts", c], state["moved", c] = rows_here, swap(rows_here)
        token[0] = rows_here

    def matmul_out(c):
        parts = tied(state["parts", c], state["moved", c])
        token[0] = state["total"] = second(
            state.get("total"), parts, down_weight, starts[c], sizes[c], down_tile
        )

    steps = [matmul_in, leave]
    steps += [pass_sum(step) for step in range(1, chips - 1)]
    steps += [finish]
    steps += [pass_hidden(step) for step in range(1, chips - 1)]
    steps += [gather, matmul_out]
    for chunk, step in queue(len(steps), gaps):
        steps[step](chunk)
    total = state["total"]

    def block_for(j):
        at = ((j // per) ^ core) * half + (j % per) * own
        return lax.dynamic_slice_in_dim(total, at, own, 0)

    result = block_for(y)
    for shift in range(1, n_gy):
        result = result + across(block_for(y ^ shift).astype(jnp.bfloat16), shift).astype(jnp.float32)
    return result


def solution(mesh):
    n_gx, n_gy = mesh.shape["gx"], mesh.shape["gy"]
    placed = (P("gy", "gx"), P("gx", "gy"), P("gx", "gy"), P("gy", "gx"))
    return jax.shard_map(
        functools.partial(local, n_gx=n_gx, n_gy=n_gy),
        mesh=mesh,
        in_specs=placed,
        out_specs=P("gy", "gx"),
        check_vma=False,
    )
```
